128 devices in a mesh: ctx: 16 (over y, z), exp: 8 (over x, core).
Axes of the slice: x: 4, y: 4, z: 4, core: 2. Of those that a mesh axis runs over, the one named last changes fastest.
Arguments:
- residual_in: bfloat16 [16384, 2048], P(('ctx', 'exp')), may hold values from -6 to 6
- queries: bfloat16 [16384, 2048], P('ctx', 'exp'), may hold values from -6 to 6
- key_rows: bfloat16 [16384, 2048], P('ctx', 'exp'), may hold values from -6 to 6
- values: bfloat16 [16384, 2048], P('ctx', 'exp'), may hold values from -6 to 6
- log_decay: float32 [16, 16384], P('exp', 'ctx'), may hold values from -1 to 0
- attn_gain: float32 [2048], P('exp'), may hold values from 0.5 to 1.5
- out_proj: bfloat16 [2048, 2048], P('exp'), may hold values from -0.125 to 0.125
- ffn_gain: float32 [2048], replicated, may hold values from 0.5 to 1.5
- router: bfloat16 [2048, 64], replicated, may hold values from -0.25 to 0.25
- route_ids: int32 [16384, 6], P(('ctx', 'exp')), may hold values from 0 to 63, as said below
- w_gate: bfloat16 [8, 2048, 1408], P('exp'), may hold values from -0.125 to 0.125
- w_up: bfloat16 [8, 2048, 1408], P('exp'), may hold values from -0.125 to 0.125
- w_down: bfloat16 [8, 1408, 2048], P('exp'), may hold values from -0.4375 to 0.4375
- shared_gate: bfloat16 [2048, 2816], P(None, 'ctx'), may hold values from -0.125 to 0.125
- shared_up: bfloat16 [2048, 2816], P(None, 'ctx'), may hold values from -0.125 to 0.125
- shared_down: bfloat16 [2816, 2048], P('ctx'), may hold values from -0.109375 to 0.109375
Outputs:
- layer_out: bfloat16 [16384, 2048], P(('ctx', 'exp'))
The draws below stay inside these ranges and needn't reach their ends.
Inputs may be any that keep to these rules, and one draw needn't show every extreme that they name: `route_ids`: each row names 6 different experts. In each aligned block of 128 rows (the rows of one device) no expert below 8 is named by more than 24 rows, and one such expert, the same in all blocks of a draw, is named by exactly 24 rows in every block.
All inputs are finite; a program needn't handle non-finite values.
Results may differ from the reference program's by a relative error of at most 0.02.
Values may be sent and summed in bfloat16 or wider, within the bound.
No kernel may reach another device: no remote copies, remote signals or barrier semaphores. Data moves between devices by JAX's collectives and lax.ppermute only.
A program may use at most 192 MiB of HBM per device.

```python
import math
import jax
import jax.numpy as jnp
from jax import lax

D = 2048
H = 16
HD = 128
ROUTED = 64
FF = 1408
SHARED = 2816
TOPK = 6
BLOCK = 512
T_DEV = 128
TOKENS = 16384
EXP_WIN = 8
HEADS_DEV = 2
SH_DEV = 176
CAP = 24
N_CTX = 16
N_EXP = 8


def shuffle_rows(perm_key, table_rows):
    return table_rows[jax.random.permutation(perm_key, T_DEV)]


def draw_route_ids(key, part):
    key = jax.random.fold_in(key, 11)
    key_pop, key_busy, key_noise, key_turn, key_perm = jax.random.split(key, 5)
    blocks = TOKENS // T_DEV
    routes_total = T_DEV * TOPK
    others = ROUTED - EXP_WIN
    lanes = jnp.arange(EXP_WIN, dtype=jnp.int32)
    busiest = jax.random.randint(key_busy, (), 0, EXP_WIN)
    popular = jnp.where(lanes == busiest, 8, jax.random.randint(key_pop, (EXP_WIN,), 1, 5))
    noise = jax.random.randint(key_noise, (blocks, EXP_WIN), -(CAP // 8), CAP // 8 + 1)
    counts = jnp.clip(popular[None, :] * CAP // 8 + noise, 0, CAP)
    counts = jnp.where(lanes[None, :] == busiest, CAP, counts)
    ends = jnp.cumsum(counts, axis=1)
    inside = ends[:, -1:]
    order = jnp.arange(routes_total, dtype=jnp.int32)[None, :]
    window_id = jnp.sum((order[:, :, None] >= ends[:, None, :]).astype(jnp.int32), axis=2)
    turn = jax.random.randint(key_turn, (blocks, 1), 0, others)
    spread = (order - inside) * others // jnp.maximum(routes_total - inside, 1)
    outer_id = EXP_WIN + (spread + turn) % others
    chosen = jnp.where(order < inside, window_id, outer_id)
    table = jnp.transpose(chosen.reshape(blocks, TOPK, T_DEV), (0, 2, 1))
    perm_keys = jax.random.split(key_perm, blocks)
    shuffled = jax.vmap(shuffle_rows)(perm_keys, table)
    return shuffled.reshape(TOKENS, TOPK).astype(jnp.int32)


def draw_log_decay(key, part):
    key = jax.random.fold_in(key, 23)
    key_kind, key_slow, key_fast, key_dev, key_rough, key_spot, key_depth = jax.random.split(key, 7)
    fast_share = 4
    slow = jnp.exp(jax.random.uniform(key_slow, (H, 1), minval=math.log(0.1), maxval=math.log(0.6)))
    fast = jax.random.randint(key_kind, (H, 1), 0, 8) < fast_share
    fast_rate = 1.0 / jax.random.uniform(key_fast, (H, 1), minval=30.0, maxval=50.0)
    rate = jnp.where(fast, fast_rate, slow / TOKENS)
    device_factor = jnp.exp(jax.random.uniform(key_dev, (H, TOKENS // T_DEV), minval=math.log(0.5), maxval=math.log(2.0)))
    device_factor = jnp.repeat(device_factor, T_DEV, axis=1)
    rough = jax.random.uniform(key_rough, (H, TOKENS), minval=0.6, maxval=1.4)
    spots = jax.random.randint(key_spot, (H, 3), 0, TOKENS)
    hits = jnp.any(jnp.arange(TOKENS, dtype=jnp.int32)[None, None, :] == spots[:, :, None], axis=1)
    depth = jax.random.uniform(key_depth, (H, TOKENS), minval=math.log(0.5), maxval=math.log(0.8))
    return (-rate * device_factor * rough + jnp.where(hits, depth, 0.0)).astype(jnp.float32)


def block_levels(own_key, shape, shards, least, high):
    def one(axis_at, blocks):
        heights = jax.random.uniform(jax.random.fold_in(jax.random.fold_in(own_key, 6), axis_at), (blocks,), jnp.float32, least / len(shards), high / len(shards))
        return jnp.repeat(jnp.exp(heights), shape[axis_at] // blocks).reshape((-1,) + (1,) * (len(shape) - axis_at - 1))

    factor_of = one(*shards[0])
    for cut in shards[1:]:
        factor_of = factor_of * one(*cut)
    return factor_of


def gaussian(rng, dims, scale, reach, cuts=(), kind=jnp.bfloat16):
    entries = scale * jax.random.normal(rng, dims, jnp.float32)
    if cuts:
        entries = entries * block_levels(rng, dims, cuts, -0.22, 0.18)
    return jnp.clip(entries, -reach, reach).astype(kind)


def setup_inputs(seed: int = 0) -> dict:
    keys = jax.random.split(jax.random.key(seed), 17)
    residual_in = gaussian(keys[0], (TOKENS, D), 1.0, 6.0, ((0, 128),))
    queries = gaussian(keys[1], (TOKENS, H * HD), 1.0, 6.0, ((0, 16), (1, 8)))
    key_rows = gaussian(keys[2], (TOKENS, H * HD), 1.0, 6.0, ((0, 16), (1, 8)))
    values = gaussian(keys[3], (TOKENS, H * HD), 1.0, 6.0, ((0, 16), (1, 8)))
    log_decay = draw_log_decay(jax.random.fold_in(keys[16], 71), 0)
    attn_gain = jnp.clip(1.0 + 0.1 * jax.random.normal(keys[5], (H * HD,), jnp.float32), 0.5, 1.5)
    out_proj = gaussian(keys[6], (H * HD, D), (H * HD) ** -0.5, 0.125, ((0, 8),))
    ffn_gain = jnp.clip(1.0 + 0.1 * jax.random.normal(keys[7], (D,), jnp.float32), 0.5, 1.5)
    router = gaussian(keys[8], (D, ROUTED), (D // 4) ** -0.5, 0.25)
    route_ids = draw_route_ids(jax.random.fold_in(keys[16], 71), 0)
    w_gate = gaussian(keys[10], (EXP_WIN, D, FF), D ** -0.5, 0.125, ((0, 8),))
    w_up = gaussian(keys[11], (EXP_WIN, D, FF), D ** -0.5, 0.125, ((0, 8),))
    w_down = gaussian(keys[12], (EXP_WIN, FF, D), (FF // 8) ** -0.5, 0.4375, ((0, 8),))
    shared_gate = gaussian(keys[13], (D, SHARED), D ** -0.5, 0.125, ((1, 16),))
    shared_up = gaussian(keys[14], (D, SHARED), D ** -0.5, 0.125, ((1, 16),))
    shared_down = gaussian(keys[15], (SHARED, D), SHARED ** -0.5, 0.109375, ((0, 16),))
    return dict(residual_in=residual_in, queries=queries, key_rows=key_rows, values=values, log_decay=log_decay, attn_gain=attn_gain, out_proj=out_proj, ffn_gain=ffn_gain, router=router, route_ids=route_ids, w_gate=w_gate, w_up=w_up, w_down=w_down, shared_gate=shared_gate, shared_up=shared_up, shared_down=shared_down)


finest = lax.Precision.HIGHEST

def attention_heads(queries, key_rows, values, log_decay):
    blocks_all = TOKENS // BLOCK
    block_shape = (blocks_all, BLOCK, H, HD)
    decay_rows = log_decay.T.reshape(blocks_all, BLOCK, H)
    causal = jnp.arange(BLOCK)[:, None] >= jnp.arange(BLOCK)[None, :]

    def advance(carried, pieces):
        query_block, key_block, value_block, decay_block = pieces
        within = jnp.cumsum(decay_block, axis=0)
        query_wide = query_block.astype(jnp.float32)
        key_plain = key_block.astype(jnp.float32)
        value_wide = value_block.astype(jnp.float32)
        scores = jnp.einsum('thd,shd->hts', query_wide, key_plain)
        spread = within.T[:, :, None] - within.T[:, None, :]
        near = jnp.where(causal, scores * jnp.exp(jnp.where(causal, spread, 0.0)), 0.0).astype(jnp.bfloat16)
        near = lax.optimization_barrier(near)
        inner = jnp.einsum('hts,shd->thd', near.astype(jnp.float32), value_wide)
        earlier = jnp.einsum('thd,hde->the', query_wide * jnp.exp(within)[:, :, None], carried, precision=finest)
        ending = within[-1]
        key_wide = key_plain * jnp.exp(ending[None, :] - within)[:, :, None]
        carried = jnp.exp(ending)[:, None, None] * carried + jnp.einsum('thd,the->hde', key_wide, value_wide, precision=finest)
        return (carried, inner + earlier)
    initial = jnp.zeros((H, HD, HD), jnp.float32)
    final_state, mixed = lax.scan(advance, initial, (queries.reshape(block_shape), key_rows.reshape(block_shape), values.reshape(block_shape), decay_rows))
    return mixed.reshape(TOKENS, H, HD)

def swiglu(rows_in, gate_w, up_w):
    gate_part = jnp.dot(rows_in, gate_w, preferred_element_type=jnp.float32)
    up_part = jnp.dot(rows_in, up_w, preferred_element_type=jnp.float32)
    return (jax.nn.silu(gate_part) * up_part).astype(jnp.bfloat16)

def reference(residual_in, queries, key_rows, values, log_decay, attn_gain, out_proj, ffn_gain, router, route_ids, w_gate, w_up, w_down, shared_gate, shared_up, shared_down):
    mixed = attention_heads(queries, key_rows, values, log_decay)
    scale = lax.rsqrt(lax.optimization_barrier(jnp.mean(mixed * mixed, axis=2, keepdims=True)) + 1e-06)
    normed = (mixed * scale * attn_gain.reshape(H, HD)).astype(jnp.bfloat16).reshape(TOKENS, H * HD)
    group_width = HEADS_DEV * HD
    attended = jnp.zeros((TOKENS, D), jnp.float32)
    for group_index in range(N_EXP):
        low_col = group_index * group_width
        part = jnp.dot(normed[:, low_col:low_col + group_width], out_proj[low_col:low_col + group_width, :], preferred_element_type=jnp.float32)
        attended = attended + lax.optimization_barrier(part.astype(jnp.bfloat16)).astype(jnp.float32)
    stream = residual_in.astype(jnp.float32) + attended
    normed_ffn = (stream * lax.rsqrt(lax.optimization_barrier(jnp.mean(stream * stream, axis=1, keepdims=True)) + 1e-06) * ffn_gain).astype(jnp.bfloat16)
    affinity = jax.nn.sigmoid(jnp.dot(normed_ffn, router, preferred_element_type=jnp.float32))
    picked = jnp.take_along_axis(affinity, route_ids, axis=1)
    gates = picked / lax.optimization_barrier(jnp.sum(picked, axis=1, keepdims=True))
    blocks_dev = TOKENS // T_DEV
    slots_all = blocks_dev * CAP
    ids_blocks = route_ids.reshape(blocks_dev, T_DEV * TOPK)
    owner_hits = (ids_blocks[:, :, None] == jnp.arange(EXP_WIN, dtype=jnp.int32)[None, None, :]).astype(jnp.int32)
    ranks = lax.optimization_barrier(jnp.sum((jnp.cumsum(owner_hits, axis=1) - owner_hits) * owner_hits, axis=2))
    block_index = jnp.arange(blocks_dev, dtype=jnp.int32)[:, None]
    places = jnp.where(ids_blocks < EXP_WIN, ids_blocks * slots_all + block_index * CAP + ranks, EXP_WIN * slots_all).astype(jnp.int32).reshape(TOKENS, TOPK)
    token_index = jnp.broadcast_to(jnp.arange(TOKENS, dtype=jnp.int32)[:, None], (TOKENS, TOPK))
    table = jnp.full((EXP_WIN * slots_all + 1,), TOKENS, jnp.int32).at[places.reshape(-1)].set(token_index.reshape(-1))
    padded_rows = jnp.concatenate([normed_ffn, jnp.zeros((1, D), jnp.bfloat16)], axis=0)
    gathered_rows = padded_rows[table[:-1]].reshape(EXP_WIN, slots_all, D)

    def one_expert(operands):
        rows_in, gate_w, up_w, down_w = operands
        hidden = swiglu(rows_in, gate_w, up_w)
        return jnp.dot(hidden, down_w, preferred_element_type=jnp.float32).astype(jnp.bfloat16)
    expert_out = lax.map(one_expert, (gathered_rows, w_gate, w_up, w_down))
    padded_out = jnp.concatenate([expert_out.reshape(EXP_WIN * slots_all, D), jnp.zeros((1, D), jnp.bfloat16)], axis=0)
    padded_out = lax.optimization_barrier(padded_out)
    routed = jnp.zeros((TOKENS, D), jnp.float32)
    for slot_index in range(TOPK):
        routed = routed + gates[:, slot_index:slot_index + 1] * padded_out[places[:, slot_index]].astype(jnp.float32)
    shared_mid = swiglu(normed_ffn, shared_gate, shared_up)
    shared_out = jnp.zeros((TOKENS, D), jnp.float32)
    for group_index in range(N_CTX):
        low_col = group_index * SH_DEV
        part = jnp.dot(shared_mid[:, low_col:low_col + SH_DEV], shared_down[low_col:low_col + SH_DEV, :], preferred_element_type=jnp.float32)
        shared_out = shared_out + lax.optimization_barrier(part.astype(jnp.bfloat16)).astype(jnp.float32)
    return (stream + shared_out + routed).astype(jnp.bfloat16)
```

```python
import functools

import jax
import jax.numpy as jnp
from jax import lax
from jax.experimental import pallas as pl
from jax.experimental.pallas import tpu as pltpu
from jax.sharding import Mesh, PartitionSpec as P

BF = jnp.bfloat16
F32 = jnp.float32
CHUNK = 256
CHUNKS = 4
HD = 128
HEADS = 2
CAP = 24
SLOTS = 2 * CAP
T_DEV = 128
T_CHIP = 256
ROUTED = 64
TOPK = 6
D = 2048
FF = 1408
SH = 176
HALF = 96
SHIFT = SH - HALF
MSG = 272
FINEST = lax.Precision.HIGHEST
Z = ("zh", "zl")

VM = pl.BlockSpec(memory_space=pltpu.VMEM)
SM = pl.BlockSpec(memory_space=pltpu.SMEM)


def mm(a, b, dims=((1,), (0,))):
    return lax.dot_general(a, b, (dims, ((), ())), preferred_element_type=F32)


def lower_ones():
    t = lax.broadcasted_iota(jnp.int32, (CHUNK, CHUNK), 0)
    s = lax.broadcasted_iota(jnp.int32, (CHUNK, CHUNK), 1)
    return t, s


def chunk_rows(decay_ref, j, t, s):
    part = decay_ref[:, j * CHUNK : (j + 1) * CHUNK]
    upper = jnp.where(t <= s, 1.0, 0.0)
    return lax.dot_general(
        part, upper, (((1,), (0,)), ((), ())), precision=FINEST, preferred_element_type=F32
    )


def chunk_cols(decay_ref, j, t, s):
    part = decay_ref[:, j * CHUNK : (j + 1) * CHUNK]
    lower = jnp.where(s <= t, 1.0, 0.0)
    return lax.dot_general(
        lower, part, (((1,), (1,)), ((), ())), precision=FINEST, preferred_element_type=F32
    )


def rows_of(j):
    return slice(j * CHUNK, (j + 1) * CHUNK)


def cols_of(h):
    return slice(h * HD, (h + 1) * HD)


def three_parts(x):
    hi = x.astype(BF).astype(F32)
    mid = (x - hi).astype(BF).astype(F32)
    lo = x - hi - mid
    return hi, mid, lo


def write_message(message_ref, states, totals):
    row = lax.broadcasted_iota(jnp.int32, (16, HD), 0)
    tail = jnp.zeros((16, HD), F32)
    for h in range(HEADS):
        message_ref[h * HD : (h + 1) * HD, :] = states[h].astype(BF)
        for i, piece in enumerate(three_parts(totals[h])):
            tail = jnp.where(row == 3 * h + i, piece, tail)
    message_ref[HEADS * HD : MSG, :] = tail.astype(BF)


def read_message(message_ref):
    tail = message_ref[HEADS * HD : MSG, :].astype(F32)
    out = []
    for h in range(HEADS):
        total = tail[3 * h : 3 * h + 1] + tail[3 * h + 1 : 3 * h + 2] + tail[3 * h + 2 : 3 * h + 3]
        out.append((message_ref[h * HD : (h + 1) * HD, :].astype(F32), total))
    return out


def states_kernel(key_ref, value_ref, decay_ref, states_ref, message_ref):
    t, s = lower_ones()
    states = [jnp.zeros((HD, HD), F32) for _ in range(HEADS)]
    totals = [jnp.zeros((1, 1), F32) for _ in range(HEADS)]
    for j in range(CHUNKS):
        col = chunk_cols(decay_ref, j, t, s)
        for h in range(HEADS):
            states_ref[j, h] = states[h]
            within = col[:, h : h + 1]
            last = within[CHUNK - 1 : CHUNK, :]
            keys = (key_ref[rows_of(j), cols_of(h)].astype(F32) * jnp.exp(last - within)).astype(BF)
            states[h] = jnp.exp(last) * states[h] + mm(
                keys, value_ref[rows_of(j), cols_of(h)], ((0,), (0,))
            )
            totals[h] = totals[h] + last
    write_message(message_ref, states, totals)


def row_kernel(place_ref, own_ref, one_ref, two_ref, three_ref, prefix_ref, total_ref, message_ref):
    z = place_ref[0]
    parts = [read_message(r) for r in (own_ref, one_ref, two_ref, three_ref)]
    at = [lax.rem(z - d + 4, 4) for d in range(4)]
    sums, sum_totals = [], []
    for h in range(HEADS):
        whole = jnp.zeros((HD, HD), F32)
        before = jnp.zeros((HD, HD), F32)
        whole_total = jnp.zeros((1, HD), F32)
        before_total = jnp.zeros((1, HD), F32)
        for d in range(4):
            after = jnp.zeros((1, HD), F32)
            between = jnp.zeros((1, HD), F32)
            for e in range(4):
                if e == d:
                    continue
                later = at[e] > at[d]
                after = after + jnp.where(later, parts[e][h][1], 0.0)
                between = between + jnp.where(later & (at[e] < z), parts[e][h][1], 0.0)
            whole = whole + jnp.exp(after) * parts[d][h][0]
            whole_total = whole_total + parts[d][h][1]
            if d:
                earlier = at[d] < z
                before = before + jnp.where(earlier, jnp.exp(between), 0.0) * parts[d][h][0]
                before_total = before_total + jnp.where(earlier, parts[d][h][1], 0.0)
        prefix_ref[h] = before
        total_ref[h : h + 1, :] = before_total
        sums.append(whole)
        sum_totals.append(whole_total)
    write_message(message_ref, sums, sum_totals)


def inner_kernel(query_ref, key_ref, value_ref, decay_ref, out_ref):
    t, s = lower_ones()
    causal = s <= t
    for j in range(CHUNKS):
        col = chunk_cols(decay_ref, j, t, s)
        row = chunk_rows(decay_ref, j, t, s)
        for h in range(HEADS):
            scores = mm(
                query_ref[rows_of(j), cols_of(h)], key_ref[rows_of(j), cols_of(h)], ((1,), (1,))
            )
            spread = jnp.where(causal, col[:, h : h + 1] - row[h : h + 1, :], 0.0)
            near = jnp.where(causal, scores * jnp.exp(spread), 0.0).astype(BF)
            out_ref[rows_of(j), cols_of(h)] = mm(near, value_ref[rows_of(j), cols_of(h)])


def mix_kernel(
    place_ref,
    query_ref,
    decay_ref,
    inner_ref,
    states_ref,
    prefix_ref,
    total_ref,
    one_ref,
    two_ref,
    three_ref,
    gain_ref,
    out_ref,
):
    x = place_ref[1]
    t, s = lower_ones()
    earlier = [read_message(r) for r in (one_ref, two_ref, three_ref)]
    incoming = []
    for h in range(HEADS):
        far = earlier[2][h][0]
        far = earlier[1][h][0] + jnp.exp(earlier[1][h][1]) * far
        far = earlier[0][h][0] + jnp.exp(earlier[0][h][1]) * far
        incoming.append(prefix_ref[h] + jnp.exp(total_ref[h : h + 1, :]) * far)
    passed = [jnp.zeros((1, 1), F32) for _ in range(HEADS)]
    for j in range(CHUNKS):
        col = chunk_cols(decay_ref, j, t, s)
        place = lax.rem(j - x + 4, 4)
        for h in range(HEADS):
            within = col[:, h : h + 1]
            state = (states_ref[j, h] + jnp.exp(passed[h]) * incoming[h]).astype(BF)
            reach = (query_ref[rows_of(j), cols_of(h)].astype(F32) * jnp.exp(within)).astype(BF)
            mixed = inner_ref[rows_of(j), cols_of(h)] + mm(reach, state)
            scale = lax.rsqrt(jnp.mean(mixed * mixed, axis=1, keepdims=True) + 1e-06)
            out_ref[place, :, cols_of(h)] = (mixed * scale * gain_ref[:, cols_of(h)]).astype(BF)
            passed[h] = passed[h] + within[CHUNK - 1 : CHUNK, :]


def project_kernel(place_ref, one_ref, two_ref, three_ref, own_ref, weights_ref, part_ref, sent_ref):
    x = place_ref[1]
    for n in range(4):
        cols = slice(n * 512, (n + 1) * 512)
        total = mm(own_ref[...], weights_ref[x, :, cols])
        for d, rows_ref in ((1, one_ref), (2, two_ref), (3, three_ref)):
            total += mm(rows_ref[...], weights_ref[lax.rem(x - d + 4, 4), :, cols])
        part_ref[:, cols] = total
        sent_ref[:, cols] = total.astype(BF)


def route_kernel(place_ref, ids_ref, named_ref, selector_ref):
    x, core = place_ref[1], place_ref[2]
    lane = lax.broadcasted_iota(jnp.int32, (T_CHIP, ROUTED), 1)
    named = jnp.zeros((T_CHIP, ROUTED), F32)
    for k in range(TOPK):
        named = jnp.where(ids_ref[:, k : k + 1] == lane, 1.0, named)
    named_ref[...] = named
    t, s = lower_ones()
    before = jnp.where((s < t) & ((s < T_DEV) == (t < T_DEV)), 1.0, 0.0).astype(BF)
    ranks = mm(before, named.astype(BF))
    slot_lane = lax.broadcasted_iota(jnp.int32, (T_CHIP, 4 * SLOTS), 1)
    token = lax.broadcasted_iota(jnp.int32, (T_CHIP, 1), 0)
    wanted = jnp.full((T_CHIP, 4 * SLOTS), -1, jnp.int32)
    for d in range(4):
        mine = lane == 2 * lax.rem(x + d, 4) + core
        hit = jnp.sum(jnp.where(mine, named, 0.0), axis=1, keepdims=True) > 0.5
        rank = jnp.sum(jnp.where(mine, ranks, 0.0), axis=1, keepdims=True).astype(jnp.int32)
        slot = jnp.where(hit, rank + jnp.where(token < T_DEV, 0, CAP) + d * SLOTS, -1)
        inside = (slot_lane >= d * SLOTS) & (slot_lane < (d + 1) * SLOTS)
        wanted = jnp.where(inside, slot, wanted)
    selector_ref[...] = jnp.where(wanted == slot_lane, 1.0, 0.0).astype(BF)


def norm_kernel(
    place_ref,
    residual_ref,
    part_ref,
    other_ref,
    gain_ref,
    router_ref,
    named_ref,
    selector_ref,
    stream_ref,
    normed_ref,
    outgoing_ref,
    back_ref,
):
    x, core = place_ref[1], place_ref[2]
    stream = residual_ref[...].astype(F32) + part_ref[...] + other_ref[...].astype(F32)
    scale = lax.rsqrt(jnp.mean(stream * stream, axis=1, keepdims=True) + 1e-06)
    normed_ref[...] = (stream * scale * gain_ref[...]).astype(BF)
    outgoing_ref[...] = mm(selector_ref[...], normed_ref[...], ((0,), (0,))).astype(BF)
    stream_ref[...] = stream
    logits = mm(normed_ref[...], router_ref[...])
    affinity = named_ref[...] / (1.0 + jnp.exp(-logits))
    gates = affinity / jnp.sum(affinity, axis=1, keepdims=True)
    lane = lax.broadcasted_iota(jnp.int32, (T_CHIP, ROUTED), 1)
    slot_lane = lax.broadcasted_iota(jnp.int32, (T_CHIP, 4 * SLOTS), 1)
    back = selector_ref[...].astype(F32)
    weight = jnp.zeros((T_CHIP, 4 * SLOTS), F32)
    for d in range(4):
        mine = lane == 2 * lax.rem(x + d, 4) + core
        gate = jnp.sum(jnp.where(mine, gates, 0.0), axis=1, keepdims=True)
        inside = (slot_lane >= d * SLOTS) & (slot_lane < (d + 1) * SLOTS)
        weight = jnp.where(inside, gate, weight)
    back_ref[...] = back * weight


def expert_kernel(own_ref, one_ref, two_ref, three_ref, gate_ref, up_ref, down_ref, out_ref, rows_ref, hidden_ref):
    for d, ref in enumerate((own_ref, one_ref, two_ref, three_ref)):
        rows_ref[d * SLOTS : (d + 1) * SLOTS, :] = ref[...]
    for n in range(0, FF, 256):
        cols = slice(n, min(n + 256, FF))
        gate = mm(rows_ref[...], gate_ref[:, cols])
        up = mm(rows_ref[...], up_ref[:, cols])
        hidden_ref[:, cols] = (gate / (1.0 + jnp.exp(-gate)) * up).astype(BF)
    for n in range(4):
        cols = slice(n * 512, (n + 1) * 512)
        out_ref[:, cols] = mm(hidden_ref[...], down_ref[:, cols]).astype(BF)


def expert(pieces, gate_w, up_w, down_w):
    count = 4 * SLOTS
    return pl.pallas_call(
        expert_kernel,
        in_specs=[VM] * 7,
        out_specs=VM,
        out_shape=jax.ShapeDtypeStruct((count, D), BF),
        scratch_shapes=[pltpu.VMEM((count, D), BF), pltpu.VMEM((count, FF), BF)],
        compiler_params=pltpu.CompilerParams(vmem_limit_bytes=30 * 2**20),
        cost_estimate=pl.CostEstimate(
            flops=6 * count * D * FF, bytes_accessed=6 * D * FF, transcendentals=0
        ),
        name="expert",
    )(*pieces, gate_w, up_w, down_w)


def shared_kernel(*refs):
    rows_ref, pieces, (gate_ref, up_ref, down_ref) = refs[0], refs[1:8], refs[8:11]
    out_ref, hidden_ref, stack_ref = refs[11:]
    for i, piece in enumerate(pieces):
        rows = slice(i * HALF, (i + 1) * HALF)
        gate = mm(rows_ref[...], piece[:HALF, :], ((1,), (1,)))
        up = mm(rows_ref[...], piece[HALF : 2 * HALF, :], ((1,), (1,)))
        hidden_ref[:, rows] = (gate / (1.0 + jnp.exp(-gate)) * up).astype(BF)
        stack_ref[rows, :] = piece[2 * HALF :, :]
    rows = slice(7 * HALF, 8 * HALF)
    gate = mm(rows_ref[...], gate_ref[...], ((1,), (1,)))
    up = mm(rows_ref[...], up_ref[...], ((1,), (1,)))
    hidden_ref[:, rows] = (gate / (1.0 + jnp.exp(-gate)) * up).astype(BF)
    stack_ref[rows, :] = down_ref[...]
    for n in range(4):
        cols = slice(n * 512, (n + 1) * 512)
        out_ref[:, cols] = mm(hidden_ref[...], stack_ref[:, cols])


def shared(rows, weights):
    count = rows.shape[0]
    return pl.pallas_call(
        shared_kernel,
        in_specs=[VM] * 11,
        out_specs=VM,
        out_shape=jax.ShapeDtypeStruct((count, D), F32),
        scratch_shapes=[pltpu.VMEM((count, 8 * HALF), BF), pltpu.VMEM((8 * HALF, D), BF)],
        compiler_params=pltpu.CompilerParams(vmem_limit_bytes=30 * 2**20),
        cost_estimate=pl.CostEstimate(
            flops=2 * count * 24 * HALF * D, bytes_accessed=48 * HALF * D, transcendentals=0
        ),
        name="shared",
    )(rows, *weights)


def ring(step, count=4):
    return [(i, (i + step) % count) for i in range(count)]


def later(step, count=4):
    return [(i, i + step) for i in range(count - step)]


def swap_core(a):
    return lax.ppermute(a, "core", [(0, 1), (1, 0)])


def swap_pair(a):
    return lax.ppermute(a, "zl", [(0, 1), (1, 0)])


def swap_z(a):
    return lax.ppermute(a, Z, [(0, 3), (3, 0), (1, 2), (2, 1)])


def on_device(
    residual_in,
    queries,
    key_rows,
    values,
    log_decay,
    attn_gain,
    out_proj,
    ffn_gain,
    router,
    route_ids,
    w_gate,
    w_up,
    w_down,
    shared_gate,
    shared_up,
    shared_down,
):
    core = lax.axis_index("core")
    x = lax.axis_index("x")
    z = lax.axis_index(Z)
    place = jnp.stack([z, x, core]).astype(jnp.int32)

    def in_order(own, other):
        return jnp.where(
            core == 0, jnp.concatenate([own, other], 0), jnp.concatenate([other, own], 0)
        )

    def half_of(a, which):
        return lax.dynamic_slice_in_dim(a, which * T_DEV, T_DEV, 0)

    projection = lax.all_gather(out_proj, "x")

    first = core * SHIFT
    down_half = lax.dynamic_slice_in_dim(shared_down, first, HALF, 0)
    repeated = jnp.arange(HALF)[:, None] < jnp.where(core == 0, 0, 2 * HALF - SH)
    shared_own = jnp.concatenate(
        [
            lax.dynamic_slice_in_dim(shared_gate.T, first, HALF, 0),
            lax.dynamic_slice_in_dim(shared_up.T, first, HALF, 0),
            jnp.where(repeated, jnp.zeros_like(down_half), down_half),
        ],
        0,
    )
    near_low = lax.ppermute(shared_own, "y", ring(1))
    near_high = lax.ppermute(shared_own, "y", ring(3))
    pair_own = swap_pair(shared_own)

    states, message = pl.pallas_call(
        states_kernel,
        in_specs=[VM] * 3,
        out_specs=[VM] * 2,
        out_shape=[
            jax.ShapeDtypeStruct((CHUNKS, HEADS, HD, HD), F32),
            jax.ShapeDtypeStruct((MSG, HD), BF),
        ],
        name="states",
    )(key_rows, values, log_decay)
    along_z = [lax.ppermute(message, Z, ring(d)) for d in (1, 2, 3)]
    inner = pl.pallas_call(
        inner_kernel,
        in_specs=[VM] * 4,
        out_specs=VM,
        out_shape=jax.ShapeDtypeStruct((CHUNK * CHUNKS, HEADS * HD), F32),
        cost_estimate=pl.CostEstimate(flops=10**9, bytes_accessed=3 * 2**20, transcendentals=0),
        name="inner",
    )(queries, key_rows, values, log_decay)
    prefix, prefix_total, row_message = pl.pallas_call(
        row_kernel,
        in_specs=[SM] + [VM] * 4,
        out_specs=[VM] * 3,
        out_shape=[
            jax.ShapeDtypeStruct((HEADS, HD, HD), F32),
            jax.ShapeDtypeStruct((HEADS, HD), F32),
            jax.ShapeDtypeStruct((MSG, HD), BF),
        ],
        name="row_states",
    )(place, message, *along_z)
    low_there, high_there, pair_there, _ = lax.optimization_barrier(
        (near_low, near_high, pair_own, row_message)
    )
    pair_low = lax.ppermute(pair_there, "y", ring(1))
    far_own = lax.ppermute(high_there, "y", ring(3))
    pair_high = swap_pair(high_there)
    along_y = [lax.ppermute(row_message, "y", later(d)) for d in (1, 2, 3)]
    normed = pl.pallas_call(
        mix_kernel,
        in_specs=[SM] + [VM] * 10,
        out_specs=VM,
        out_shape=jax.ShapeDtypeStruct((4, T_CHIP, HEADS * HD), BF),
        name="mix",
    )(
        place,
        queries,
        log_decay,
        inner,
        states,
        prefix,
        prefix_total,
        *along_y,
        attn_gain.reshape(1, HEADS * HD),
    )

    pair_low_there, far_there, pair_high_there, _ = lax.optimization_barrier(
        (pair_low, far_own, pair_high, normed)
    )
    last_gate = swap_pair(far_there[:HALF])
    last_up = lax.ppermute(pair_low_there[HALF : 2 * HALF], "y", ring(1))
    last_down = lax.ppermute(pair_high_there[2 * HALF :], "y", ring(3))
    shared_weights = (
        shared_own,
        near_low,
        near_high,
        pair_own,
        pair_low,
        far_own,
        pair_high,
        last_gate,
        last_up,
        last_down,
    )

    ids = in_order(route_ids, swap_core(route_ids))
    named, selector = pl.pallas_call(
        route_kernel,
        in_specs=[SM, VM],
        out_specs=[VM] * 2,
        out_shape=[
            jax.ShapeDtypeStruct((T_CHIP, ROUTED), F32),
            jax.ShapeDtypeStruct((T_CHIP, 4 * SLOTS), BF),
        ],
        name="routes",
    )(place, ids)
    residual = in_order(residual_in, swap_core(residual_in))

    heads = [lax.ppermute(normed[d], "x", ring(d)) for d in (1, 2, 3)]
    part, part_sent = pl.pallas_call(
        project_kernel,
        in_specs=[SM] + [VM] * 5,
        out_specs=[VM] * 2,
        out_shape=[
            jax.ShapeDtypeStruct((T_CHIP, D), F32),
            jax.ShapeDtypeStruct((T_CHIP, D), BF),
        ],
        name="project",
    )(place, *heads, normed[0], projection)
    stream, normed_ffn, outgoing, weights_back = pl.pallas_call(
        norm_kernel,
        in_specs=[SM] + [VM] * 7,
        out_specs=[VM] * 4,
        out_shape=[
            jax.ShapeDtypeStruct((T_CHIP, D), F32),
            jax.ShapeDtypeStruct((T_CHIP, D), BF),
            jax.ShapeDtypeStruct((4 * SLOTS, D), BF),
            jax.ShapeDtypeStruct((T_CHIP, 4 * SLOTS), F32),
        ],
        name="norm",
    )(
        place,
        residual,
        part,
        swap_core(part_sent),
        ffn_gain.reshape(1, D),
        router,
        named,
        selector,
    )

    sent = [outgoing[d * SLOTS : (d + 1) * SLOTS] for d in range(4)]
    arrived = [sent[0]] + [lax.ppermute(sent[d], "x", ring(d)) for d in (1, 2, 3)]

    partner_own = swap_z(half_of(normed_ffn, core))
    partner_rows = in_order(partner_own, swap_core(partner_own))

    result = expert(arrived, w_gate[0], w_up[0], w_down[0])
    returned = [result[:SLOTS]] + [
        lax.ppermute(result[d * SLOTS : (d + 1) * SLOTS], "x", ring(4 - d)) for d in (1, 2, 3)
    ]

    partner_part = shared(partner_rows, shared_weights)
    partner_sum = half_of(partner_part, core) + swap_core(
        half_of(partner_part, 1 - core).astype(BF)
    ).astype(F32)
    from_partner = swap_z(partner_sum.astype(BF)).astype(F32)
    own_part = shared(normed_ffn, shared_weights)

    high = weights_back.astype(BF)
    low = (weights_back - high.astype(F32)).astype(BF)
    back = jnp.concatenate(returned, 0)
    both = own_part + mm(high, back) + mm(low, back)
    other = swap_core(half_of(both, 1 - core).astype(BF)).astype(F32)
    return (half_of(stream, core) + half_of(both, core) + other + from_partner).astype(BF)


def solution(mesh):
    fine = Mesh(mesh.devices.reshape(4, 2, 2, 4, 2), ("y", "zh", "zl", "x", "core"))
    ctx = ("y", "zh", "zl")
    exp = ("x", "core")
    return jax.shard_map(
        on_device,
        mesh=fine,
        in_specs=(
            P(ctx + exp, None),
            P(ctx, exp),
            P(ctx, exp),
            P(ctx, exp),
            P(exp, ctx),
            P(exp),
            P(exp, None),
            P(),
            P(),
            P(ctx + exp, None),
            P(exp, None, None),
            P(exp, None, None),
            P(exp, None, None),
            P(None, ctx),
            P(None, ctx),
            P(ctx, None),
        ),
        out_specs=P(ctx + exp, None),
        check_vma=False,
    )
```

```python
import functools
import math

import jax
import jax.numpy as jnp
from jax import lax
from jax.experimental import pallas as pl
from jax.experimental.pallas import tpu as pltpu
from jax.sharding import Mesh, PartitionSpec as P

BF = jnp.bfloat16
F32 = jnp.float32
CHUNK = 256
CHUNKS = 4
HD = 128
HEADS = 2
CAP = 24
SLOTS = 2 * CAP
T_DEV = 128
T_CHIP = 256
ROUTED = 64
TOPK = 6
D = 2048
FF = 1408
SH = 176
PART = 48
LAST = SH - PART
N_CTX = 16
MSG = 272
FINEST = lax.Precision.HIGHEST

VM = pl.BlockSpec(memory_space=pltpu.VMEM)
HBM = pl.BlockSpec(memory_space=pltpu.HBM)
SM = pl.BlockSpec(memory_space=pltpu.SMEM)


def mm(a, b, dims=((1,), (0,))):
    return lax.dot_general(a, b, (dims, ((), ())), preferred_element_type=F32)


def places():
    t = lax.broadcasted_iota(jnp.int32, (CHUNK, CHUNK), 0)
    s = lax.broadcasted_iota(jnp.int32, (CHUNK, CHUNK), 1)
    return t, s


def split_decay(decay_ref):
    rows = jnp.concatenate(
        [decay_ref[:, j * CHUNK : (j + 1) * CHUNK] for j in range(CHUNKS)], axis=0
    )
    return jnp.concatenate(three_parts(rows), axis=0).astype(BF)


def chunk_cols(decay_ref, t, s):
    lower = jnp.where(s <= t, 1.0, 0.0).astype(BF)
    out = mm(lower, split_decay(decay_ref), ((1,), (1,)))
    n = CHUNKS * HEADS
    return out[:, :n] + out[:, n : 2 * n] + out[:, 2 * n :]


def chunk_rows(decay_ref, t, s):
    upper = jnp.where(t <= s, 1.0, 0.0).astype(BF)
    out = mm(split_decay(decay_ref), upper)
    n = CHUNKS * HEADS
    return out[:n] + out[n : 2 * n] + out[2 * n :]


def rows_of(j):
    return slice(j * CHUNK, (j + 1) * CHUNK)


def cols_of(h):
    return slice(h * HD, (h + 1) * HD)


def three_parts(x):
    hi = x.astype(BF).astype(F32)
    mid = (x - hi).astype(BF).astype(F32)
    lo = x - hi - mid
    return hi, mid, lo


def write_message(message_ref, states, totals):
    row = lax.broadcasted_iota(jnp.int32, (16, HD), 0)
    tail = jnp.zeros((16, HD), F32)
    for h in range(HEADS):
        message_ref[h * HD : (h + 1) * HD, :] = states[h].astype(BF)
        for i, piece in enumerate(three_parts(totals[h])):
            tail = jnp.where(row == 3 * h + i, piece, tail)
    message_ref[HEADS * HD : MSG, :] = tail.astype(BF)


def read_message(message_ref):
    tail = message_ref[HEADS * HD : MSG, :].astype(F32)
    out = []
    for h in range(HEADS):
        total = tail[3 * h : 3 * h + 1] + tail[3 * h + 1 : 3 * h + 2] + tail[3 * h + 2 : 3 * h + 3]
        out.append((message_ref[h * HD : (h + 1) * HD, :].astype(F32), total))
    return out


def states_kernel(
    place_ref, decay_ref, key_ref, value_ref, gate_ref, up_ref, down_ref,
    states_ref, passed_ref, message_ref, slab_ref, keys_ref, values_ref, sems
):
    loads = [
        [
            pltpu.make_async_copy(ref.at[rows_of(j)], buffer.at[rows_of(j)], sems.at[k, j])
            for k, (ref, buffer) in enumerate(((key_ref, keys_ref), (value_ref, values_ref)))
        ]
        for j in range(CHUNKS)
    ]
    first = pl.ds(pl.multiple_of(place_ref[6], 16), PART)
    cuts = [
        pltpu.make_async_copy(ref.at[first], slab_ref.at[i], sems.at[2, i])
        for i, ref in enumerate((gate_ref, up_ref, down_ref))
    ]
    for pair in loads:
        for copy in pair:
            copy.start()
    for copy in cuts:
        copy.start()
    t, s = places()
    within = chunk_cols(decay_ref, t, s)
    last = within[CHUNK - 1 : CHUNK, :]
    rest = jnp.exp(last - within)
    states = [jnp.zeros((HD, HD), F32) for _ in range(HEADS)]
    totals = [jnp.zeros((1, HD), F32) for _ in range(HEADS)]
    for j in range(CHUNKS):
        for copy in loads[j]:
            copy.wait()
        for h in range(HEADS):
            states_ref[j, h] = states[h]
            passed_ref[j, h : h + 1, :] = jnp.exp(totals[h])
            at = HEADS * j + h
            ending = jnp.broadcast_to(last[:, at : at + 1], (1, HD))
            keys = (keys_ref[rows_of(j), cols_of(h)].astype(F32) * rest[:, at : at + 1]).astype(BF)
            states[h] = jnp.exp(ending) * states[h] + mm(
                keys, values_ref[rows_of(j), cols_of(h)], ((0,), (0,))
            )
            totals[h] = totals[h] + ending
    write_message(message_ref, states, totals)
    for copy in cuts:
        copy.wait()


def step_kernel(bit, place_ref, own_ref, other_ref, *rest):
    before, (prefix_ref, total_ref, message_ref) = rest[:-3], rest[-3:]
    upper = place_ref[bit] == 1
    own, other = read_message(own_ref), read_message(other_ref)
    states, totals = [], []
    for h in range(HEADS):
        (mine, mine_total), (theirs, theirs_total) = own[h], other[h]
        if before:
            prefix, total = before[0][h], before[1][h : h + 1, :]
            prefix_ref[h] = jnp.where(upper, jnp.exp(total) * theirs + prefix, prefix)
            total_ref[h : h + 1, :] = jnp.where(upper, theirs_total + total, total)
        else:
            prefix_ref[h] = jnp.where(upper, theirs, 0.0)
            total_ref[h : h + 1, :] = jnp.where(upper, theirs_total, 0.0)
        first = jnp.where(upper, theirs, mine)
        second = jnp.where(upper, mine, theirs)
        states.append(jnp.exp(jnp.where(upper, mine_total, theirs_total)) * first + second)
        totals.append(mine_total + theirs_total)
    write_message(message_ref, states, totals)


def inner_kernel(query_ref, key_ref, value_ref, decay_ref, out_ref):
    t, s = places()
    causal = s <= t
    cols = chunk_cols(decay_ref, t, s)
    rows = chunk_rows(decay_ref, t, s)
    for j in range(CHUNKS):
        for h in range(HEADS):
            at = HEADS * j + h
            scores = mm(
                query_ref[rows_of(j), cols_of(h)], key_ref[rows_of(j), cols_of(h)], ((1,), (1,))
            )
            spread = jnp.where(causal, cols[:, at : at + 1] - rows[at : at + 1, :], -1e30)
            near = (scores * jnp.exp(spread)).astype(BF)
            out_ref[rows_of(j), cols_of(h)] = mm(near, value_ref[rows_of(j), cols_of(h)])


def mix_kernel(
    place_ref,
    query_ref,
    decay_ref,
    inner_ref,
    states_ref,
    passed_ref,
    prefix_ref,
    total_ref,
    other_ref,
    gain_ref,
    *outs,
):
    x = place_ref[4]
    t, s = places()
    other = read_message(other_ref)
    incoming = []
    for h in range(HEADS):
        far = jnp.exp(total_ref[h : h + 1, :]) * other[h][0] + prefix_ref[h]
        incoming.append(jnp.where(place_ref[3] == 1, far, prefix_ref[h]))
    lower = jnp.where(s <= t, 1.0, 0.0).astype(BF)
    for d in range(CHUNKS):
        j = lax.rem(x + d, 4)
        rows = pl.ds(pl.multiple_of(j * CHUNK, CHUNK), CHUNK)
        parts = jnp.concatenate(three_parts(decay_ref[:, rows]), axis=0).astype(BF)
        summed = mm(lower, parts, ((1,), (1,)))
        reach = jnp.exp(summed[:, :HEADS] + summed[:, HEADS : 2 * HEADS] + summed[:, 2 * HEADS :])
        for h in range(HEADS):
            state = (states_ref[j, h] + passed_ref[j, h : h + 1, :] * incoming[h]).astype(BF)
            query = (query_ref[rows, cols_of(h)].astype(F32) * reach[:, h : h + 1]).astype(BF)
            mixed = inner_ref[rows, cols_of(h)] + mm(query, state)
            scale = lax.rsqrt(jnp.mean(mixed * mixed, axis=1, keepdims=True) + 1e-06)
            outs[d][:, cols_of(h)] = (mixed * scale * gain_ref[:, cols_of(h)]).astype(BF)


def project_kernel(
    place_ref, own_ref, one_ref, two_ref, three_ref, residual_ref, w0_ref, w1_ref, w2a_ref, w2b_ref, w3_ref,
    part_ref, sent_ref, rows_ref
):
    core = place_ref[5]
    mine = pl.ds(pl.multiple_of(core * T_DEV, T_DEV), T_DEV)
    theirs = pl.ds(pl.multiple_of((1 - core) * T_DEV, T_DEV), T_DEV)
    for d, ref in enumerate((own_ref, one_ref, two_ref, three_ref)):
        cols = slice(d * CHUNK, (d + 1) * CHUNK)
        rows_ref[:T_DEV, cols] = ref[mine, :]
        rows_ref[T_DEV:, cols] = ref[theirs, :]
    for n in range(4):
        cols = slice(n * 512, (n + 1) * 512)
        total = jnp.zeros((T_CHIP, 512), F32)
        at = 0
        for ref in (w0_ref, w1_ref, w2a_ref, w2b_ref, w3_ref):
            total += mm(rows_ref[:, at : at + ref.shape[0]], ref[:, cols])
            at += ref.shape[0]
        own = total[:T_DEV] + residual_ref[:, cols].astype(F32)
        part_ref[:T_DEV, cols] = own
        part_ref[T_DEV:, cols] = total[T_DEV:]
        sent_ref[:T_DEV, cols] = total[T_DEV:].astype(BF)
        sent_ref[T_DEV:, cols] = own.astype(BF)


def route_kernel(place_ref, own_ref, other_ref, named_ref, selector_ref):
    x, core = place_ref[4], place_ref[5]
    lane = lax.broadcasted_iota(jnp.int32, (T_CHIP, ROUTED), 1)
    ids = jnp.concatenate([own_ref[...], other_ref[...]], axis=0)
    named = jnp.zeros((T_CHIP, ROUTED), F32)
    for k in range(TOPK):
        named = jnp.where(ids[:, k : k + 1] == lane, 1.0, named)
    named_ref[...] = named
    t, s = places()
    before = jnp.where((s < t) & ((s < T_DEV) == (t < T_DEV)), 1.0, 0.0).astype(BF)
    ranks = mm(before, named.astype(BF))
    slot_lane = lax.broadcasted_iota(jnp.int32, (T_CHIP, 4 * SLOTS), 1)
    token = lax.broadcasted_iota(jnp.int32, (T_CHIP, 1), 0)
    wanted = jnp.full((T_CHIP, 4 * SLOTS), -1, jnp.int32)
    for d in range(4):
        mine = lane == 2 * lax.rem(x + d, 4) + core
        hit = jnp.sum(jnp.where(mine, named, 0.0), axis=1, keepdims=True) > 0.5
        rank = jnp.sum(jnp.where(mine, ranks, 0.0), axis=1, keepdims=True).astype(jnp.int32)
        slot = jnp.where(hit, rank + jnp.where(token < T_DEV, 0, CAP) + d * SLOTS, -1)
        inside = (slot_lane >= d * SLOTS) & (slot_lane < (d + 1) * SLOTS)
        wanted = jnp.where(inside, slot, wanted)
    selector_ref[...] = jnp.where(wanted == slot_lane, 1.0, 0.0).astype(BF)


def norm_kernel(
    place_ref,
    part_ref,
    other_ref,
    gain_ref,
    router_ref,
    named_ref,
    selector_ref,
    stream_ref,
    mine_ref,
    theirs_ref,
    out0_ref,
    out1_ref,
    out2_ref,
    out3_ref,
    back_ref,
    normed_ref,
):
    x, core = place_ref[4], place_ref[5]
    for half, out in ((0, mine_ref), (1, theirs_ref)):
        rows = slice(half * T_DEV, (half + 1) * T_DEV)
        stream = part_ref[rows, :] + other_ref[rows, :].astype(F32)
        if half == 0:
            stream_ref[...] = stream
        scale = lax.rsqrt(jnp.mean(stream * stream, axis=1, keepdims=True) + 1e-06)
        normed = (stream * scale * gain_ref[...]).astype(BF)
        normed_ref[rows, :] = normed
        out[...] = normed
    sent = mm(selector_ref[...], normed_ref[...], ((0,), (0,))).astype(BF)
    for d, ref in enumerate((out0_ref, out1_ref, out2_ref, out3_ref)):
        ref[...] = sent[d * SLOTS : (d + 1) * SLOTS]
    logits = mm(normed_ref[...], router_ref[...], ((1,), (1,)))
    affinity = named_ref[...] / (1.0 + jnp.exp(-logits))
    gates = affinity / jnp.sum(affinity, axis=1, keepdims=True)
    lane = lax.broadcasted_iota(jnp.int32, (T_CHIP, ROUTED), 1)
    slot_lane = lax.broadcasted_iota(jnp.int32, (T_CHIP, 4 * SLOTS), 1)
    weight = jnp.zeros((T_CHIP, 4 * SLOTS), F32)
    for d in range(4):
        mine = lane == 2 * lax.rem(x + d, 4) + core
        gate = jnp.sum(jnp.where(mine, gates, 0.0), axis=1, keepdims=True)
        inside = (slot_lane >= d * SLOTS) & (slot_lane < (d + 1) * SLOTS)
        weight = jnp.where(inside, gate, weight)
    weight = selector_ref[...].astype(F32) * weight
    high = weight.astype(BF)
    back_ref[:, : 4 * SLOTS] = high
    back_ref[:, 4 * SLOTS :] = (weight - high.astype(F32)).astype(BF)


def load_kernel(*refs):
    count = len(refs) // 2
    copies = [
        pltpu.make_async_copy(refs[i], refs[count + i], refs[-1].at[i]) for i in range(count)
    ]
    for copy in copies:
        copy.start()
    for copy in copies:
        copy.wait()


def expert_kernel(
    own_ref, one_ref, two_ref, three_ref, gate_ref, up_ref, down_ref, *rest
):
    outs, (rows_ref, hidden_ref) = rest[:4], rest[4:]
    for d, ref in enumerate((own_ref, one_ref, two_ref, three_ref)):
        rows_ref[d * SLOTS : (d + 1) * SLOTS, :] = ref[...]
    for n in range(0, FF, 256):
        cols = slice(n, min(n + 256, FF))
        gate = mm(rows_ref[...], gate_ref[:, cols])
        up = mm(rows_ref[...], up_ref[:, cols])
        hidden_ref[:, cols] = (gate / (1.0 + jnp.exp(-gate)) * up).astype(BF)
    for n in range(4):
        cols = slice(n * 512, (n + 1) * 512)
        out = mm(hidden_ref[...], down_ref[:, cols]).astype(BF)
        for d, ref in enumerate(outs):
            ref[:, cols] = out[d * SLOTS : (d + 1) * SLOTS]


def shared_kernel(place_ref, own_ref, other_ref, weights_ref, mine_ref, theirs_ref, rows_ref, side_ref):
    rows_ref[:, :T_DEV] = own_ref[...].T
    rows_ref[:, T_DEV:] = other_ref[...].T

    def side(k):
        return weights_ref[:, k].reshape(N_CTX * PART, D)

    gate = mm(side(0), rows_ref[...])
    up = mm(side(1), rows_ref[...])
    unit = lax.rem(lax.broadcasted_iota(jnp.int32, (N_CTX * PART, T_CHIP), 0), PART)
    kept = unit >= jnp.where(place_ref[6] == LAST, 4 * PART - SH, 0)
    side_ref[...] = jnp.where(kept, gate / (1.0 + jnp.exp(-gate)) * up, 0.0).astype(BF)
    hidden = side_ref[...].T
    for n in range(4):
        cols = slice(n * 512, (n + 1) * 512)
        out = mm(hidden, weights_ref[:, 2, :, cols].reshape(N_CTX * PART, 512))
        mine_ref[:, cols] = out[:T_DEV]
        theirs_ref[:, cols] = out[T_DEV:].astype(BF)


def combine_kernel(mine_ref, theirs_ref, back_ref, one_ref, two_ref, three_ref, four_ref, out_ref, sent_ref, rows_ref):
    for d, ref in enumerate((one_ref, two_ref, three_ref, four_ref)):
        rows_ref[d * SLOTS : (d + 1) * SLOTS, :] = ref[...]
    for n in range(4):
        cols = slice(n * 512, (n + 1) * 512)
        routed = mm(back_ref[:, : 4 * SLOTS], rows_ref[:, cols]) + mm(
            back_ref[:, 4 * SLOTS :], rows_ref[:, cols]
        )
        out_ref[:, cols] = mine_ref[:, cols] + routed[:T_DEV]
        sent_ref[:, cols] = (theirs_ref[:, cols].astype(F32) + routed[T_DEV:]).astype(BF)


def call(kernel, outs, *args, scratch=(), scalars=0, loose=0, sems=None, limit=12, name=None, flops=10**9):
    size = sum(a.size * a.dtype.itemsize for a in args)
    size += sum(math.prod(shape) * jnp.dtype(kind).itemsize for shape, kind in outs)
    if not flops:
        size = 0
    sems = [] if sems is None else [pltpu.SemaphoreType.DMA(sems)]
    return pl.pallas_call(
        kernel,
        in_specs=[SM] * scalars + [VM] * (len(args) - scalars - loose) + [HBM] * loose,
        out_specs=[VM] * len(outs),
        out_shape=[jax.ShapeDtypeStruct(shape, kind) for shape, kind in outs],
        scratch_shapes=[pltpu.VMEM(shape, kind) for shape, kind in scratch] + sems,
        compiler_params=pltpu.CompilerParams(vmem_limit_bytes=limit * 2**20),
        cost_estimate=pl.CostEstimate(flops=flops, bytes_accessed=size, transcendentals=0),
        name=name or kernel.__name__.replace("_kernel", ""),
    )(*args)


def group(*values):
    return lax.optimization_barrier(values)


def after(value, *others):
    return lax.optimization_barrier((value,) + others)[0]


def ring(step, count=4):
    return [(i, (i + step) % count) for i in range(count)]


def swap_core(a):
    return lax.ppermute(a, "core", [(0, 1), (1, 0)])


def swap(a, axis, bit):
    count = 4 if axis == "y" or axis == "x" else 2
    return lax.ppermute(a, axis, [(i, i ^ bit) for i in range(count)])


def on_device(
    residual_in,
    queries,
    key_rows,
    values,
    log_decay,
    attn_gain,
    out_proj,
    ffn_gain,
    router,
    route_ids,
    w_gate,
    w_up,
    w_down,
    shared_gate,
    shared_up,
    shared_down,
):
    core = lax.axis_index("core")
    x = lax.axis_index("x")
    y = lax.axis_index("y")
    first = jnp.minimum((2 * lax.rem(x, 2) + core) * PART, LAST)
    place = jnp.stack(
        [lax.axis_index("zl"), lax.axis_index("zh"), lax.rem(y, 2), y // 2, x, core, first]
    ).astype(jnp.int32)
    token_rows = ((T_DEV, D), BF)

    proj_low = lax.ppermute(out_proj, "x", ring(1))
    proj_high = lax.ppermute(out_proj, "x", ring(3))

    states, passed, message, slab = call(
        states_kernel,
        [
            ((CHUNKS, HEADS, HD, HD), F32),
            ((CHUNKS, HEADS, HD), F32),
            ((MSG, HD), BF),
            ((3, PART, D), BF),
        ],
        place,
        log_decay,
        key_rows,
        values,
        shared_gate.T,
        shared_up.T,
        shared_down,
        scratch=[((CHUNK * CHUNKS, HEADS * HD), BF)] * 2,
        scalars=1,
        loose=5,
        sems=(3, 4),
        limit=60,
    )
    shared_weights = lax.all_gather(slab, ("y", "zh", "zl"))
    prefix = ()
    for bit, (axis, step) in enumerate((("zl", 1), ("zh", 1), ("y", 1))):
        other = swap(message, axis, step)
        *prefix, message = call(
            functools.partial(step_kernel, bit),
            [((HEADS, HD, HD), F32), ((HEADS, HD), F32), ((MSG, HD), BF)],
            place,
            message,
            other,
            *prefix,
            scalars=1,
            name=f"step{bit}",
        )
        if bit == 0:
            other_ids = swap_core(after(route_ids, message))
            (inner,) = call(
                inner_kernel,
                [((CHUNK * CHUNKS, HEADS * HD), F32)],
                after(queries, message),
                key_rows,
                values,
                log_decay,
            )
        if bit == 1:
            named, selector = call(
                route_kernel,
                [((T_CHIP, ROUTED), F32), ((T_CHIP, 4 * SLOTS), BF)],
                place,
                after(route_ids, message, inner),
                other_ids,
                scalars=1,
            )
    other = swap(message, "y", 2)
    far_low, far_high = after(proj_low, message)[:T_DEV], after(proj_high, message)[T_DEV:]
    other, far_low, far_high, named, selector = group(other, far_low, far_high, named, selector)
    normed = call(
        mix_kernel,
        [((T_CHIP, HEADS * HD), BF)] * 4,
        place,
        queries,
        log_decay,
        inner,
        states,
        passed,
        *prefix,
        other,
        attn_gain.reshape(1, HEADS * HD),
        scalars=1,
    )

    proj_far_low = lax.ppermute(far_low, "x", ring(1))
    proj_far_high = lax.ppermute(far_high, "x", ring(3))
    heads = [lax.ppermute(normed[d], "x", ring(d)) for d in (1, 2, 3)]

    *heads, proj_far_low, proj_far_high = group(*heads, proj_far_low, proj_far_high)

    part, part_sent = call(
        project_kernel,
        [((T_CHIP, D), F32), ((T_CHIP, D), BF)],
        place,
        normed[0],
        *heads,
        residual_in,
        out_proj,
        proj_low,
        proj_far_low,
        proj_far_high,
        proj_high,
        scratch=[((T_CHIP, 4 * CHUNK), BF)],
        scalars=1,
        flops=6 * 10**9,
    )
    stream, mine, theirs, *outgoing, back = call(
        norm_kernel,
        [((T_DEV, D), F32), token_rows, token_rows]
        + [((SLOTS, D), BF)] * 4
        + [((T_CHIP, 8 * SLOTS), BF)],
        place,
        part,
        swap_core(part_sent),
        ffn_gain.reshape(1, D),
        router.T,
        named,
        selector,
        scratch=[((T_CHIP, D), BF)],
        scalars=1,
        flops=3 * 10**10,
    )
    arrived = [lax.ppermute(outgoing[d], "x", ring(d)) for d in (1, 2, 3)]
    expert_weights = call(
        load_kernel,
        [((D, FF), BF), ((D, FF), BF), ((FF, D), BF)],
        after(w_gate, mine)[0],
        w_up[0],
        w_down[0],
        loose=3,
        sems=(3,),
        limit=28,
    )
    *arrived, gate_w, up_w, down_w = group(*arrived, *expert_weights)
    partner_mine = swap(after(mine, *arrived), "x", 1)
    results = call(
        expert_kernel,
        [((SLOTS, D), BF)] * 4,
        outgoing[0],
        *arrived,
        gate_w,
        up_w,
        down_w,
        scratch=[((4 * SLOTS, D), BF), ((4 * SLOTS, FF), BF)],
    )
    returned = [lax.ppermute(results[d], "x", ring(4 - d)) for d in (1, 2, 3)]

    (shared_here,) = call(
        load_kernel,
        [((N_CTX, 3, PART, D), BF)],
        after(shared_weights, *results),
        loose=1,
        sems=(1,),
        limit=24,
        flops=0,
    )
    partner_mine, shared_here, *returned = group(partner_mine, shared_here, *returned)
    partner_theirs = swap_core(partner_mine)

    def shared(own, other):
        return call(
            shared_kernel,
            [((T_DEV, D), F32), token_rows],
            place,
            own,
            other,
            shared_here,
            scratch=[((D, T_CHIP), BF), ((N_CTX * PART, T_CHIP), BF)],
            scalars=1,
            flops=0,
        )

    partner_kept, partner_sent = shared(partner_mine, partner_theirs)
    partner_other = swap_core(partner_sent)
    partner_sum = partner_kept + partner_other.astype(F32)
    from_partner = swap(partner_sum.astype(BF), "x", 1)
    own_kept, own_sent = shared(after(mine, partner_other), theirs)
    kept, sent = call(
        combine_kernel,
        [((T_DEV, D), F32), token_rows],
        own_kept,
        own_sent,
        back,
        results[0],
        *returned,
        scratch=[((4 * SLOTS, D), BF)],
        flops=0,
    )
    return (stream + kept + swap_core(after(sent, from_partner)).astype(F32) + from_partner.astype(F32)).astype(BF)


def solution(mesh):
    fine = Mesh(mesh.devices.reshape(4, 2, 2, 4, 2), ("y", "zh", "zl", "x", "core"))
    ctx = ("y", "zh", "zl")
    exp = ("x", "core")
    return jax.shard_map(
        on_device,
        mesh=fine,
        in_specs=(
            P(ctx + exp, None),
            P(ctx, exp),
            P(ctx, exp),
            P(ctx, exp),
            P(exp, ctx),
            P(exp),
            P(exp, None),
            P(),
            P(),
            P(ctx + exp, None),
            P(exp, None, None),
            P(exp, None, None),
            P(exp, None, None),
            P(None, ctx),
            P(None, ctx),
            P(ctx, None),
        ),
        out_specs=P(ctx + exp, None),
        check_vma=False,
    )
```

```python
import functools
import math

import jax
import jax.numpy as jnp
from jax import lax
from jax.experimental import pallas as pl
from jax.experimental.pallas import tpu as pltpu
from jax.sharding import Mesh, PartitionSpec as P

BF = jnp.bfloat16
F32 = jnp.float32
CHUNK = 256
CHUNKS = 4
HD = 128
HEADS = 2
CAP = 24
SLOTS = 2 * CAP
T_DEV = 128
T_CHIP = 256
ROUTED = 64
TOPK = 6
D = 2048
FF = 1408
SH = 176
PART = 48
LAST = SH - PART
N_CTX = 16
MSG = 272
FINEST = lax.Precision.HIGHEST

VM = pl.BlockSpec(memory_space=pltpu.VMEM)
HBM = pl.BlockSpec(memory_space=pltpu.HBM)
SM = pl.BlockSpec(memory_space=pltpu.SMEM)


def mm(a, b, dims=((1,), (0,))):
    return lax.dot_general(a, b, (dims, ((), ())), preferred_element_type=F32)


def places():
    t = lax.broadcasted_iota(jnp.int32, (CHUNK, CHUNK), 0)
    s = lax.broadcasted_iota(jnp.int32, (CHUNK, CHUNK), 1)
    return t, s


def split_decay(decay_ref):
    rows = jnp.concatenate(
        [decay_ref[:, j * CHUNK : (j + 1) * CHUNK] for j in range(CHUNKS)], axis=0
    )
    return jnp.concatenate(three_parts(rows), axis=0).astype(BF)


def chunk_cols(decay_ref, t, s):
    lower = jnp.where(s <= t, 1.0, 0.0).astype(BF)
    out = mm(lower, split_decay(decay_ref), ((1,), (1,)))
    n = CHUNKS * HEADS
    return out[:, :n] + out[:, n : 2 * n] + out[:, 2 * n :]


def chunk_rows(decay_ref, t, s):
    upper = jnp.where(t <= s, 1.0, 0.0).astype(BF)
    out = mm(split_decay(decay_ref), upper)
    n = CHUNKS * HEADS
    return out[:n] + out[n : 2 * n] + out[2 * n :]


def rows_of(j):
    return slice(j * CHUNK, (j + 1) * CHUNK)


def cols_of(h):
    return slice(h * HD, (h + 1) * HD)


def three_parts(x):
    hi = x.astype(BF).astype(F32)
    mid = (x - hi).astype(BF).astype(F32)
    lo = x - hi - mid
    return hi, mid, lo


def write_message(message_ref, states, totals):
    row = lax.broadcasted_iota(jnp.int32, (16, HD), 0)
    tail = jnp.zeros((16, HD), F32)
    for h in range(HEADS):
        message_ref[h * HD : (h + 1) * HD, :] = states[h].astype(BF)
        for i, piece in enumerate(three_parts(totals[h])):
            tail = jnp.where(row == 3 * h + i, piece, tail)
    message_ref[HEADS * HD : MSG, :] = tail.astype(BF)


def read_message(message_ref):
    tail = message_ref[HEADS * HD : MSG, :].astype(F32)
    out = []
    for h in range(HEADS):
        total = tail[3 * h : 3 * h + 1] + tail[3 * h + 1 : 3 * h + 2] + tail[3 * h + 2 : 3 * h + 3]
        out.append((message_ref[h * HD : (h + 1) * HD, :].astype(F32), total))
    return out


def states_kernel(
    place_ref, decay_ref, key_ref, value_ref, gate_ref, up_ref, down_ref,
    states_ref, passed_ref, message_ref, slab_ref, keys_ref, values_ref, sems
):
    loads = [
        [
            pltpu.make_async_copy(ref.at[rows_of(j)], buffer.at[rows_of(j)], sems.at[k, j])
            for k, (ref, buffer) in enumerate(((key_ref, keys_ref), (value_ref, values_ref)))
        ]
        for j in range(CHUNKS)
    ]
    first = pl.ds(pl.multiple_of(place_ref[6], 16), PART)
    cuts = [
        pltpu.make_async_copy(ref.at[first], slab_ref.at[i], sems.at[2, i])
        for i, ref in enumerate((gate_ref, up_ref, down_ref))
    ]
    for pair in loads:
        for copy in pair:
            copy.start()
    for copy in cuts:
        copy.start()
    t, s = places()
    within = chunk_cols(decay_ref, t, s)
    last = within[CHUNK - 1 : CHUNK, :]
    rest = jnp.exp(last - within)
    states = [jnp.zeros((HD, HD), F32) for _ in range(HEADS)]
    totals = [jnp.zeros((1, HD), F32) for _ in range(HEADS)]
    for j in range(CHUNKS):
        for copy in loads[j]:
            copy.wait()
        for h in range(HEADS):
            states_ref[j, h] = states[h]
            passed_ref[j, h : h + 1, :] = jnp.exp(totals[h])
            at = HEADS * j + h
            ending = jnp.broadcast_to(last[:, at : at + 1], (1, HD))
            keys = (keys_ref[rows_of(j), cols_of(h)].astype(F32) * rest[:, at : at + 1]).astype(BF)
            states[h] = jnp.exp(ending) * states[h] + mm(
                keys, values_ref[rows_of(j), cols_of(h)], ((0,), (0,))
            )
            totals[h] = totals[h] + ending
    write_message(message_ref, states, totals)
    for copy in cuts:
        copy.wait()


def step_kernel(bit, place_ref, own_ref, other_ref, *rest):
    before, (prefix_ref, total_ref, message_ref) = rest[:-3], rest[-3:]
    upper = place_ref[bit] == 1
    own, other = read_message(own_ref), read_message(other_ref)
    states, totals = [], []
    for h in range(HEADS):
        (mine, mine_total), (theirs, theirs_total) = own[h], other[h]
        if before:
            prefix, total = before[0][h], before[1][h : h + 1, :]
            prefix_ref[h] = jnp.where(upper, jnp.exp(total) * theirs + prefix, prefix)
            total_ref[h : h + 1, :] = jnp.where(upper, theirs_total + total, total)
        else:
            prefix_ref[h] = jnp.where(upper, theirs, 0.0)
            total_ref[h : h + 1, :] = jnp.where(upper, theirs_total, 0.0)
        first = jnp.where(upper, theirs, mine)
        second = jnp.where(upper, mine, theirs)
        states.append(jnp.exp(jnp.where(upper, mine_total, theirs_total)) * first + second)
        totals.append(mine_total + theirs_total)
    write_message(message_ref, states, totals)


def inner_kernel(query_ref, key_ref, value_ref, decay_ref, out_ref):
    t, s = places()
    causal = s <= t
    cols = chunk_cols(decay_ref, t, s)
    rows = chunk_rows(decay_ref, t, s)
    for j in range(CHUNKS):
        for h in range(HEADS):
            at = HEADS * j + h
            scores = mm(
                query_ref[rows_of(j), cols_of(h)], key_ref[rows_of(j), cols_of(h)], ((1,), (1,))
            )
            spread = jnp.where(causal, cols[:, at : at + 1] - rows[at : at + 1, :], -1e30)
            near = (scores * jnp.exp(spread)).astype(BF)
            out_ref[rows_of(j), cols_of(h)] = mm(near, value_ref[rows_of(j), cols_of(h)])


def mix_kernel(
    place_ref,
    query_ref,
    decay_ref,
    inner_ref,
    states_ref,
    passed_ref,
    prefix_ref,
    total_ref,
    other_ref,
    gain_ref,
    *outs,
):
    x = place_ref[4]
    t, s = places()
    other = read_message(other_ref)
    incoming = []
    for h in range(HEADS):
        far = jnp.exp(total_ref[h : h + 1, :]) * other[h][0] + prefix_ref[h]
        incoming.append(jnp.where(place_ref[3] == 1, far, prefix_ref[h]))
    lower = jnp.where(s <= t, 1.0, 0.0).astype(BF)
    for d in range(CHUNKS):
        j = lax.rem(x + d, 4)
        rows = pl.ds(pl.multiple_of(j * CHUNK, CHUNK), CHUNK)
        parts = jnp.concatenate(three_parts(decay_ref[:, rows]), axis=0).astype(BF)
        summed = mm(lower, parts, ((1,), (1,)))
        reach = jnp.exp(summed[:, :HEADS] + summed[:, HEADS : 2 * HEADS] + summed[:, 2 * HEADS :])
        for h in range(HEADS):
            state = (states_ref[j, h] + passed_ref[j, h : h + 1, :] * incoming[h]).astype(BF)
            query = (query_ref[rows, cols_of(h)].astype(F32) * reach[:, h : h + 1]).astype(BF)
            mixed = inner_ref[rows, cols_of(h)] + mm(query, state)
            scale = lax.rsqrt(jnp.mean(mixed * mixed, axis=1, keepdims=True) + 1e-06)
            outs[d][:, cols_of(h)] = (mixed * scale * gain_ref[:, cols_of(h)]).astype(BF)


def project_kernel(
    place_ref, own_ref, one_ref, two_ref, three_ref, residual_ref, w0_ref, w1_ref, w2a_ref, w2b_ref, w3_ref,
    part_ref, sent_ref, rows_ref
):
    core = place_ref[5]
    mine = pl.ds(pl.multiple_of(core * T_DEV, T_DEV), T_DEV)
    theirs = pl.ds(pl.multiple_of((1 - core) * T_DEV, T_DEV), T_DEV)
    for d, ref in enumerate((own_ref, one_ref, two_ref, three_ref)):
        cols = slice(d * CHUNK, (d + 1) * CHUNK)
        rows_ref[:T_DEV, cols] = ref[mine, :]
        rows_ref[T_DEV:, cols] = ref[theirs, :]
    for n in range(4):
        cols = slice(n * 512, (n + 1) * 512)
        total = jnp.zeros((T_CHIP, 512), F32)
        at = 0
        for ref in (w0_ref, w1_ref, w2a_ref, w2b_ref, w3_ref):
            total += mm(rows_ref[:, at : at + ref.shape[0]], ref[:, cols])
            at += ref.shape[0]
        own = total[:T_DEV] + residual_ref[:, cols].astype(F32)
        part_ref[:T_DEV, cols] = own
        part_ref[T_DEV:, cols] = total[T_DEV:]
        sent_ref[:T_DEV, cols] = total[T_DEV:].astype(BF)
        sent_ref[T_DEV:, cols] = own.astype(BF)


def route_kernel(place_ref, own_ref, other_ref, named_ref, selector_ref):
    x, core = place_ref[4], place_ref[5]
    lane = lax.broadcasted_iota(jnp.int32, (T_CHIP, ROUTED), 1)
    ids = jnp.concatenate([own_ref[...], other_ref[...]], axis=0)
    named = jnp.zeros((T_CHIP, ROUTED), F32)
    for k in range(TOPK):
        named = jnp.where(ids[:, k : k + 1] == lane, 1.0, named)
    named_ref[...] = named
    t, s = places()
    before = jnp.where((s < t) & ((s < T_DEV) == (t < T_DEV)), 1.0, 0.0).astype(BF)
    ranks = mm(before, named.astype(BF))
    slot_lane = lax.broadcasted_iota(jnp.int32, (T_CHIP, 4 * SLOTS), 1)
    token = lax.broadcasted_iota(jnp.int32, (T_CHIP, 1), 0)
    wanted = jnp.full((T_CHIP, 4 * SLOTS), -1, jnp.int32)
    for d in range(4):
        mine = lane == 2 * lax.rem(x + d, 4) + core
        hit = jnp.sum(jnp.where(mine, named, 0.0), axis=1, keepdims=True) > 0.5
        rank = jnp.sum(jnp.where(mine, ranks, 0.0), axis=1, keepdims=True).astype(jnp.int32)
        slot = jnp.where(hit, rank + jnp.where(token < T_DEV, 0, CAP) + d * SLOTS, -1)
        inside = (slot_lane >= d * SLOTS) & (slot_lane < (d + 1) * SLOTS)
        wanted = jnp.where(inside, slot, wanted)
    selector_ref[...] = jnp.where(wanted == slot_lane, 1.0, 0.0).astype(BF)


def norm_kernel(
    place_ref,
    part_ref,
    other_ref,
    gain_ref,
    router_ref,
    named_ref,
    selector_ref,
    stream_ref,
    mine_ref,
    theirs_ref,
    out0_ref,
    out1_ref,
    out2_ref,
    out3_ref,
    back_ref,
    normed_ref,
):
    x, core = place_ref[4], place_ref[5]
    for half, out in ((0, mine_ref), (1, theirs_ref)):
        rows = slice(half * T_DEV, (half + 1) * T_DEV)
        stream = part_ref[rows, :] + other_ref[rows, :].astype(F32)
        if half == 0:
            stream_ref[...] = stream
        scale = lax.rsqrt(jnp.mean(stream * stream, axis=1, keepdims=True) + 1e-06)
        normed = (stream * scale * gain_ref[...]).astype(BF)
        normed_ref[rows, :] = normed
        out[...] = normed
    sent = mm(selector_ref[...], normed_ref[...], ((0,), (0,))).astype(BF)
    for d, ref in enumerate((out0_ref, out1_ref, out2_ref, out3_ref)):
        ref[...] = sent[d * SLOTS : (d + 1) * SLOTS]
    logits = mm(normed_ref[...], router_ref[...], ((1,), (1,)))
    affinity = named_ref[...] / (1.0 + jnp.exp(-logits))
    gates = affinity / jnp.sum(affinity, axis=1, keepdims=True)
    lane = lax.broadcasted_iota(jnp.int32, (T_CHIP, ROUTED), 1)
    slot_lane = lax.broadcasted_iota(jnp.int32, (T_CHIP, 4 * SLOTS), 1)
    weight = jnp.zeros((T_CHIP, 4 * SLOTS), F32)
    for d in range(4):
        mine = lane == 2 * lax.rem(x + d, 4) + core
        gate = jnp.sum(jnp.where(mine, gates, 0.0), axis=1, keepdims=True)
        inside = (slot_lane >= d * SLOTS) & (slot_lane < (d + 1) * SLOTS)
        weight = jnp.where(inside, gate, weight)
    weight = selector_ref[...].astype(F32) * weight
    high = weight.astype(BF)
    back_ref[:, : 4 * SLOTS] = high
    back_ref[:, 4 * SLOTS :] = (weight - high.astype(F32)).astype(BF)


def load_kernel(*refs):
    count = len(refs) // 2
    copies = [
        pltpu.make_async_copy(refs[i], refs[count + i], refs[-1].at[i]) for i in range(count)
    ]
    for copy in copies:
        copy.start()
    for copy in copies:
        copy.wait()


def expert_kernel(
    own_ref, one_ref, two_ref, three_ref, gate_ref, up_ref, down_ref, *rest
):
    outs, (rows_ref, hidden_ref) = rest[:4], rest[4:]
    for d, ref in enumerate((own_ref, one_ref, two_ref, three_ref)):
        rows_ref[d * SLOTS : (d + 1) * SLOTS, :] = ref[...]
    for n in range(0, FF, 256):
        cols = slice(n, min(n + 256, FF))
        gate = mm(rows_ref[...], gate_ref[:, cols])
        up = mm(rows_ref[...], up_ref[:, cols])
        hidden_ref[:, cols] = (gate / (1.0 + jnp.exp(-gate)) * up).astype(BF)
    for n in range(4):
        cols = slice(n * 512, (n + 1) * 512)
        out = mm(hidden_ref[...], down_ref[:, cols]).astype(BF)
        for d, ref in enumerate(outs):
            ref[:, cols] = out[d * SLOTS : (d + 1) * SLOTS]


def shared_kernel(place_ref, own_ref, other_ref, weights_ref, mine_ref, theirs_ref, rows_ref, side_ref):
    rows_ref[:, :T_DEV] = own_ref[...].T
    rows_ref[:, T_DEV:] = other_ref[...].T

    def side(k):
        return weights_ref[:, k].reshape(N_CTX * PART, D)

    gate = mm(side(0), rows_ref[...])
    up = mm(side(1), rows_ref[...])
    unit = lax.rem(lax.broadcasted_iota(jnp.int32, (N_CTX * PART, T_CHIP), 0), PART)
    kept = unit >= jnp.where(place_ref[6] == LAST, 4 * PART - SH, 0)
    side_ref[...] = jnp.where(kept, gate / (1.0 + jnp.exp(-gate)) * up, 0.0).astype(BF)
    hidden = side_ref[...].T
    for n in range(4):
        cols = slice(n * 512, (n + 1) * 512)
        out = mm(hidden, weights_ref[:, 2, :, cols].reshape(N_CTX * PART, 512))
        mine_ref[:, cols] = out[:T_DEV]
        theirs_ref[:, cols] = out[T_DEV:].astype(BF)


def combine_kernel(mine_ref, theirs_ref, back_ref, one_ref, two_ref, three_ref, four_ref, out_ref, sent_ref, rows_ref):
    for d, ref in enumerate((one_ref, two_ref, three_ref, four_ref)):
        rows_ref[d * SLOTS : (d + 1) * SLOTS, :] = ref[...]
    for n in range(4):
        cols = slice(n * 512, (n + 1) * 512)
        routed = mm(back_ref[:, : 4 * SLOTS], rows_ref[:, cols]) + mm(
            back_ref[:, 4 * SLOTS :], rows_ref[:, cols]
        )
        out_ref[:, cols] = mine_ref[:, cols] + routed[:T_DEV]
        sent_ref[:, cols] = (theirs_ref[:, cols].astype(F32) + routed[T_DEV:]).astype(BF)


def call(kernel, outs, *args, scratch=(), scalars=0, loose=0, sems=None, limit=12, name=None, flops=10**9):
    size = sum(a.size * a.dtype.itemsize for a in args)
    size += sum(math.prod(shape) * jnp.dtype(kind).itemsize for shape, kind in outs)
    if not flops:
        size = 0
    sems = [] if sems is None else [pltpu.SemaphoreType.DMA(sems)]
    return pl.pallas_call(
        kernel,
        in_specs=[SM] * scalars + [VM] * (len(args) - scalars - loose) + [HBM] * loose,
        out_specs=[VM] * len(outs),
        out_shape=[jax.ShapeDtypeStruct(shape, kind) for shape, kind in outs],
        scratch_shapes=[pltpu.VMEM(shape, kind) for shape, kind in scratch] + sems,
        compiler_params=pltpu.CompilerParams(vmem_limit_bytes=limit * 2**20),
        cost_estimate=pl.CostEstimate(flops=flops, bytes_accessed=size, transcendentals=0),
        name=name or kernel.__name__.replace("_kernel", ""),
    )(*args)


def group(*values):
    return lax.optimization_barrier(values)


def after(value, *others):
    return lax.optimization_barrier((value,) + others)[0]


def ring(step, count=4):
    return [(i, (i + step) % count) for i in range(count)]


def swap_core(a):
    return lax.ppermute(a, "core", [(0, 1), (1, 0)])


def swap(a, axis, bit):
    count = 4 if axis == "y" or axis == "x" else 2
    return lax.ppermute(a, axis, [(i, i ^ bit) for i in range(count)])


def on_device(
    residual_in,
    queries,
    key_rows,
    values,
    log_decay,
    attn_gain,
    out_proj,
    ffn_gain,
    router,
    route_ids,
    w_gate,
    w_up,
    w_down,
    shared_gate,
    shared_up,
    shared_down,
):
    core = lax.axis_index("core")
    x = lax.axis_index("x")
    y = lax.axis_index("y")
    first = jnp.minimum((2 * lax.rem(x, 2) + core) * PART, LAST)
    place = jnp.stack(
        [lax.axis_index("zl"), lax.axis_index("zh"), lax.rem(y, 2), y // 2, x, core, first]
    ).astype(jnp.int32)
    token_rows = ((T_DEV, D), BF)

    proj_low = lax.ppermute(out_proj, "x", ring(1))
    proj_high = lax.ppermute(out_proj, "x", ring(3))

    other_ids = swap_core(route_ids)

    states, passed, message, slab = call(
        states_kernel,
        [
            ((CHUNKS, HEADS, HD, HD), F32),
            ((CHUNKS, HEADS, HD), F32),
            ((MSG, HD), BF),
            ((3, PART, D), BF),
        ],
        after(place, other_ids),
        log_decay,
        key_rows,
        values,
        shared_gate.T,
        shared_up.T,
        shared_down,
        scratch=[((CHUNK * CHUNKS, HEADS * HD), BF)] * 2,
        scalars=1,
        loose=5,
        sems=(3, 4),
        limit=60,
    )
    shared_weights = lax.all_gather(slab, ("y", "zh", "zl"))
    prefix = ()
    for bit, (axis, step) in enumerate((("zl", 1), ("zh", 1), ("y", 1))):
        other = swap(message, axis, step)
        *prefix, message = call(
            functools.partial(step_kernel, bit),
            [((HEADS, HD, HD), F32), ((HEADS, HD), F32), ((MSG, HD), BF)],
            place,
            message,
            other,
            *prefix,
            scalars=1,
            name=f"step{bit}",
        )
        if bit == 0:
            (inner,) = call(
                inner_kernel,
                [((CHUNK * CHUNKS, HEADS * HD), F32)],
                after(queries, message),
                key_rows,
                values,
                log_decay,
            )
        if bit == 1:
            named, selector = call(
                route_kernel,
                [((T_CHIP, ROUTED), F32), ((T_CHIP, 4 * SLOTS), BF)],
                place,
                after(route_ids, message, inner),
                other_ids,
                scalars=1,
            )
    other = swap(message, "y", 2)
    far_low, far_high = after(proj_low, message)[:T_DEV], after(proj_high, message)[T_DEV:]
    other, far_low, far_high, named, selector = group(other, far_low, far_high, named, selector)
    normed = call(
        mix_kernel,
        [((T_CHIP, HEADS * HD), BF)] * 4,
        place,
        queries,
        log_decay,
        inner,
        states,
        passed,
        *prefix,
        other,
        attn_gain.reshape(1, HEADS * HD),
        scalars=1,
    )

    proj_far_low = lax.ppermute(far_low, "x", ring(1))
    proj_far_high = lax.ppermute(far_high, "x", ring(3))
    heads = [lax.ppermute(normed[d], "x", ring(d)) for d in (1, 2, 3)]

    *heads, proj_far_low, proj_far_high = group(*heads, proj_far_low, proj_far_high)

    part, part_sent = call(
        project_kernel,
        [((T_CHIP, D), F32), ((T_CHIP, D), BF)],
        place,
        normed[0],
        *heads,
        residual_in,
        out_proj,
        proj_low,
        proj_far_low,
        proj_far_high,
        proj_high,
        scratch=[((T_CHIP, 4 * CHUNK), BF)],
        scalars=1,
        flops=6 * 10**9,
    )
    stream, mine, theirs, *outgoing, back = call(
        norm_kernel,
        [((T_DEV, D), F32), token_rows, token_rows]
        + [((SLOTS, D), BF)] * 4
        + [((T_CHIP, 8 * SLOTS), BF)],
        place,
        part,
        swap_core(part_sent),
        ffn_gain.reshape(1, D),
        router.T,
        named,
        selector,
        scratch=[((T_CHIP, D), BF)],
        scalars=1,
        flops=3 * 10**10,
    )
    arrived = [lax.ppermute(outgoing[d], "x", ring(d)) for d in (1, 2, 3)]
    expert_weights = call(
        load_kernel,
        [((D, FF), BF), ((D, FF), BF), ((FF, D), BF)],
        after(w_gate, mine)[0],
        w_up[0],
        w_down[0],
        loose=3,
        sems=(3,),
        limit=28,
    )
    *arrived, gate_w, up_w, down_w = group(*arrived, *expert_weights)
    partner_mine = swap(after(mine, *arrived), "x", 1)
    results = call(
        expert_kernel,
        [((SLOTS, D), BF)] * 4,
        outgoing[0],
        *arrived,
        gate_w,
        up_w,
        down_w,
        scratch=[((4 * SLOTS, D), BF), ((4 * SLOTS, FF), BF)],
    )
    returned = [lax.ppermute(results[d], "x", ring(4 - d)) for d in (1, 2, 3)]

    (shared_here,) = call(
        load_kernel,
        [((N_CTX, 3, PART, D), BF)],
        after(shared_weights, *results),
        loose=1,
        sems=(1,),
        limit=24,
        flops=0,
    )
    partner_mine, shared_here, *returned = group(partner_mine, shared_here, *returned)
    partner_theirs = swap_core(partner_mine)

    def shared(own, other):
        return call(
            shared_kernel,
            [((T_DEV, D), F32), token_rows],
            place,
            own,
            other,
            shared_here,
            scratch=[((D, T_CHIP), BF), ((N_CTX * PART, T_CHIP), BF)],
            scalars=1,
            flops=0,
        )

    partner_kept, partner_sent = shared(partner_mine, partner_theirs)
    partner_other = swap_core(partner_sent)
    partner_sum = partner_kept + partner_other.astype(F32)
    from_partner = swap(partner_sum.astype(BF), "x", 1)
    own_kept, own_sent = shared(after(mine, partner_other), theirs)
    kept, sent = call(
        combine_kernel,
        [((T_DEV, D), F32), token_rows],
        own_kept,
        own_sent,
        back,
        results[0],
        *returned,
        scratch=[((4 * SLOTS, D), BF)],
        flops=0,
    )
    return (stream + kept + swap_core(after(sent, from_partner)).astype(F32) + from_partner.astype(F32)).astype(BF)


def solution(mesh):
    fine = Mesh(mesh.devices.reshape(4, 2, 2, 4, 2), ("y", "zh", "zl", "x", "core"))
    ctx = ("y", "zh", "zl")
    exp = ("x", "core")
    return jax.shard_map(
        on_device,
        mesh=fine,
        in_specs=(
            P(ctx + exp, None),
            P(ctx, exp),
            P(ctx, exp),
            P(ctx, exp),
            P(exp, ctx),
            P(exp),
            P(exp, None),
            P(),
            P(),
            P(ctx + exp, None),
            P(exp, None, None),
            P(exp, None, None),
            P(exp, None, None),
            P(None, ctx),
            P(None, ctx),
            P(ctx, None),
        ),
        out_specs=P(ctx + exp, None),
        check_vma=False,
    )
```
